32 devices in a mesh: grp: 2 (over x), blk: 16 (over z, y, core).
Axes of the slice: x: 2, y: 2, z: 4, core: 2. Of those that a mesh axis runs over, the one named last changes fastest.
Arguments:
- queries: float32 [16384, 1024], P(('grp', 'blk')), parts along dimension 0, may hold values from -24 to 24
- passages: float32 [16384, 1024], P(('grp', 'blk')), parts along dimension 0, may hold values from -6 to 6
- pattern: int32 [64, 8], P(('grp', 'blk')), parts along dimension 0, may hold values from -1 to 31, as said below
- teacher: bfloat16 [64, 8, 256, 256], P(('grp', 'blk')), parts along dimension 0, may hold values from -20 to 370
Outputs:
- row_loss: float32 [16384], P(('grp', 'blk')), parts along dimension 0
- query_grad: float32 [16384, 1024], P(('grp', 'blk')), parts along dimension 0
- passage_grad: float32 [16384, 1024], P(('grp', 'blk')), parts along dimension 0
The draws below stay inside these ranges and needn't reach their ends.
There are 2 independent parts, one for each index of `grp`. The reference program is written for one: setup_inputs(seed, part) draws one part's arguments, and reference() takes and returns one part's arrays. A program takes and returns all parts, laid end to end along the dimension named above; each array names one. Nothing has to cross between parts.
Inputs may be any that keep to these rules, and one draw needn't show every extreme that they name: Every entry of pattern[g] is -1 or a passage group held by a device of blk within 2 of the device holding query group g, counted around the closed axis; the live entries of a row come first and are distinct; every row has one live entry or more, and some row has 8.
All inputs are finite; a program needn't handle non-finite values.
Results may differ from the reference program's by a relative error of at most 0.0003.
Values sent between devices are 32-bit elements; how exact they have to be, the bound alone decides.
A program may use at most 128 MiB of HBM per device.

```python
import math
import jax
import jax.numpy as jnp
from jax import lax

D = 1024
G = 256
K = 8
REACH = 2
PG_DEV = 2
QG_DEV = 2
QGROUPS = 32
PGROUPS = 32


def pattern_of(key):
    candidates = (2 * REACH + 1) * PG_DEV
    cycle_devices = PGROUPS // PG_DEV
    row_keys = jax.random.split(jax.random.fold_in(key, 11), QGROUPS)
    picked = jax.vmap(lambda one_key: jax.random.permutation(one_key, candidates)[:K])(row_keys)
    counts = jax.random.randint(jax.random.fold_in(key, 12), (QGROUPS,), 1, K + 1)
    group_ids = jnp.arange(QGROUPS)
    counts = jnp.where(group_ids == 0, K, counts)
    device_of = group_ids // QG_DEV
    offset = picked // PG_DEV - REACH
    within = picked % PG_DEV
    target_group = (device_of[:, None] + offset) % cycle_devices * PG_DEV + within
    is_live = jnp.arange(K)[None, :] < counts[:, None]
    return jnp.where(is_live, target_group, -1).astype(jnp.int32)


def passages_of(key):
    sub_key = jax.random.fold_in(key, 21)
    values = jnp.clip(jax.random.normal(sub_key, (PGROUPS * G, D), jnp.float32), -6.0, 6.0)
    return values


def draw_pattern(key, part):
    return pattern_of(key)


def draw_passages(key, part):
    return passages_of(key)


def draw_queries(key, part):
    sub_key = jax.random.fold_in(key, 31)
    values = jnp.clip(jax.random.normal(sub_key, (QGROUPS, G, D), jnp.float32), -6.0, 6.0)
    return values.reshape(QGROUPS * G, D)


def draw_teacher(key, part):
    sub_key = jax.random.fold_in(key, 41)
    shape = (QGROUPS, K, G, G)
    values = jnp.clip(3.0 * jax.random.normal(sub_key, shape, jnp.float32), -18.0, 18.0)
    return values.astype(jnp.bfloat16)


def setup_inputs(seed: int = 0, part: int = 0) -> dict:
    splits = jax.random.split(jax.random.key(seed), 5)
    part_splits = jax.random.split(jax.random.fold_in(splits[4], part), 5)
    queries = draw_queries(jax.random.fold_in(jax.random.fold_in(splits[4], part), 71), part)
    passages = draw_passages(jax.random.fold_in(jax.random.fold_in(splits[4], part), 71), part)
    pattern = draw_pattern(jax.random.fold_in(jax.random.fold_in(splits[4], part), 71), part)
    teacher = draw_teacher(jax.random.fold_in(jax.random.fold_in(splits[4], part), 71), part)
    return dict(queries=queries, passages=passages, pattern=pattern, teacher=teacher)


def reference(queries, passages, pattern, teacher):
    score_scale = 2.0 / math.sqrt(D)
    passage_groups = passages.reshape(PGROUPS, G, D)
    query_groups = queries.reshape(QGROUPS, G, D)

    def visit(carry, inputs):
        query_rows, slot_list, labels = inputs
        is_live = slot_list >= 0
        slot_index = jnp.where(is_live, slot_list, 0).astype(jnp.int32)
        chosen = passage_groups[slot_index]
        scores = jnp.einsum('rd,kcd->krc', query_rows, chosen, precision=lax.Precision.HIGHEST) * score_scale
        live = is_live[:, None, None]
        student = jnp.where(live, scores, -jnp.inf)
        top_student = lax.optimization_barrier(jnp.max(student, axis=(0, 2), keepdims=True))
        exp_student = jnp.exp(student - top_student)
        sum_student = lax.optimization_barrier(jnp.sum(exp_student, axis=(0, 2), keepdims=True))
        probs = exp_student / sum_student
        log_probs = student - top_student - jnp.log(sum_student)
        logits = jnp.where(live, labels.astype(jnp.float32), -jnp.inf)
        top_teacher = lax.optimization_barrier(jnp.max(logits, axis=(0, 2), keepdims=True))
        exp_teacher = jnp.exp(logits - top_teacher)
        sum_teacher = lax.optimization_barrier(jnp.sum(exp_teacher, axis=(0, 2), keepdims=True))
        target = exp_teacher / sum_teacher
        log_target = logits - top_teacher - jnp.log(sum_teacher)
        terms = jnp.where(live, target * (log_target - log_probs), 0.0)
        losses = lax.optimization_barrier(jnp.sum(terms, axis=(0, 2)))
        grads = jnp.where(live, probs - target, 0.0) * score_scale
        query_grad = jnp.einsum('krc,kcd->rd', grads, chosen, precision=lax.Precision.HIGHEST)
        tile_grad = jnp.einsum('krc,rd->kcd', grads, query_rows, precision=lax.Precision.HIGHEST)
        carry = carry.at[slot_index].add(tile_grad)
        return (carry, (losses, query_grad))
    initial = jnp.zeros((PGROUPS, G, D), jnp.float32)
    total, (losses, query_grads) = lax.scan(visit, initial, (query_groups, pattern, teacher))
    return (losses.reshape(-1), query_grads.reshape(-1, D), total.reshape(-1, D))
```

```python
import functools
import math

import jax
import jax.numpy as jnp
from jax import lax
from jax.experimental import pallas as pl
from jax.experimental.pallas import tpu as pltpu
from jax.sharding import PartitionSpec as P

CHUNKS = 8
DEAD = -1e30
SIB, YB, ZB, FB, OWN = range(5)
F32 = jnp.float32
BF16 = jnp.bfloat16
MESH = pl.DeviceIdType.MESH


def split(x):
    hi = x.astype(BF16)
    return hi, (x - hi.astype(F32)).astype(BF16)


def dot(a, b, ca, cb):
    return lax.dot_general(a, b, (((ca,), (cb,)), ((), ())), preferred_element_type=F32)


def dot3(ah, al, bh, bl, ca, cb):
    return dot(ah, bh, ca, cb) + (dot(al, bh, ca, cb) + dot(ah, bl, ca, cb))


def fold(x, op):
    rows, cols = x.shape
    return op(x.reshape(rows // 8, 8, cols), axis=0)


def kernel(
    n, pat, q, p, teach, loss, qg, pg,
    win, wh, wl, qh, ql, st, tg, gh, gl, rec, stat, kk, cap,
    s1, r1, s2, r2,
):
    rows, width = q.shape
    groups, slots, size, _ = teach.shape
    scale = 2.0 / math.sqrt(width)
    part = lax.axis_index("grp")
    me = lax.axis_index("blk")
    chip, core = me // 2, me % 2
    odd = chip % 2
    to = 1 - 2 * odd
    wrap = lambda i: lax.rem(i + n, n)
    sib = me + 1 - 2 * core
    ypart = me + 2 * to
    znext = wrap(me + 4 * to)
    zprev = wrap(me - 4 * to)
    owners = [sib, ypart, wrap(me - 2 * to), wrap(me + 2 * core - 1), me]
    fwd_y = core == odd
    z_gets = core != odd

    barrier = pltpu.get_barrier_semaphore()
    for d in (sib, ypart, znext, zprev):
        pl.semaphore_signal(barrier, inc=1, device_id=(part, d), device_id_type=MESH)
    pl.semaphore_wait(barrier, 4)

    def copy(src, dst, ss, rs, kind, i, dev):
        return pltpu.make_async_remote_copy(
            src_ref=src, dst_ref=dst, send_sem=ss.at[kind, i], recv_sem=rs.at[kind, i],
            device_id=(part, dev), device_id_type=MESH,
        )

    step = rows // CHUNKS
    half = CHUNKS // 2
    piece = lambda i: pl.ds(i * step, step)
    group = lambda j: pl.ds(j * size, size)

    g_sib = lambda i: copy(p.at[piece(i)], win.at[SIB, piece(i)], s1, r1, SIB, i, sib)
    g_y = lambda i: copy(p.at[piece(i)], win.at[YB, piece(i)], s1, r1, YB, i, ypart)
    g_z = lambda i: copy(win.at[YB, piece(i)], win.at[ZB, piece(i)], s1, r1, ZB, i, znext)
    g_f = lambda b, i: copy(win.at[b, piece(i)], win.at[FB, piece(i)], s1, r1, FB, i, sib)
    t_sib = lambda i: copy(win.at[SIB, piece(i)], rec.at[SIB, piece(i)], s2, r2, SIB, i, sib)
    t_y = lambda i: copy(win.at[YB, piece(i)], rec.at[YB, piece(i)], s2, r2, YB, i, ypart)
    t_z = lambda i: copy(win.at[ZB, piece(i)], rec.at[ZB, piece(i)], s2, r2, ZB, i, zprev)
    t_f = lambda i: copy(win.at[FB, piece(i)], rec.at[FB, piece(i)], s2, r2, FB, i, sib)

    for i in range(CHUNKS):
        g_y(i).start()
    for i in range(CHUNKS):
        g_sib(i).start()

    for b in range(5):
        for j in range(2):
            wanted = owners[b] * 2 + j
            for g in range(groups):
                slot, live = jnp.int32(0), jnp.int32(0)
                for k in range(slots):
                    hit = (pat[g, k] == wanted).astype(jnp.int32)
                    slot = jnp.maximum(slot, hit * k)
                    live = jnp.maximum(live, hit)
                kk[(g * 5 + b) * 2 + j] = slot
                alive = live.astype(F32)
                cap[(g * 5 + b) * 2 + j] = 3e38 * alive + DEAD * (1.0 - alive)

    stat[...] = jnp.full(stat.shape, DEAD, F32)

    def split_rows(src, hi, lo, count, strip=32):
        def one(t, _):
            r = pl.ds(pl.multiple_of(t * strip, strip), strip)
            h, l = split(src[r, :])
            hi[r, :] = h
            lo[r, :] = l
            return 0
        lax.fori_loop(0, count // strip, one, 0)

    def score(b, j):
        src = p.at[group(j)] if b == OWN else win.at[b, group(j)]
        split_rows(src, wh.at[b, group(j)], wl.at[b, group(j)], size)
        for g in range(groups):
            cols = pl.ds(g * size, size)
            s = dot3(wh[b, group(j), :], wl[b, group(j), :], qh[group(g), :], ql[group(g), :], 1, 1)
            s = jnp.minimum(s * scale, cap[(g * 5 + b) * 2 + j])
            st[b, group(j), cols] = s
            stat[0:8, cols] = jnp.maximum(stat[0:8, cols], fold(s, jnp.max))

    def teacher(b):
        def one(t, _):
            g, j = t // 2, t % 2
            at = (g * 5 + b) * 2 + j
            x = teach[g, kk[at]].astype(F32).T
            x = jnp.minimum(x, cap[at])
            r = pl.ds(pl.multiple_of(j * size, size), size)
            c = pl.ds(pl.multiple_of(g * size, size), size)
            tg[b, r, c] = x
            stat[8:16, c] = jnp.maximum(stat[8:16, c], fold(x, jnp.max))
            return 0
        lax.fori_loop(0, groups * 2, one, 0)

    strip = 64
    per = rows // strip

    def teacher_sums(lo, hi, top):
        def one(t, carry):
            z, d = carry
            r = pl.ds(pl.multiple_of((t % per) * strip, strip), strip)
            x = tg[t // per, r, :] - top
            e = jnp.exp(x)
            tg[t // per, r, :] = e
            return z + fold(e, jnp.sum), d + fold(e * x, jnp.sum)
        zero = jnp.zeros((8, rows), F32)
        z, d = lax.fori_loop(lo * per, hi * per, one, (zero, zero))
        stat[16:24, :] = z
        stat[24:32, :] = d

    def all_teacher():
        teacher_sums(0, 5, jnp.max(stat[8:16, :], axis=0, keepdims=True))

    work = [
        lambda: (split_rows(q, qh, ql, rows), score(OWN, 0)),
        lambda: (score(OWN, 1), [g_sib(i).wait_recv() for i in range(CHUNKS)]),
        lambda: score(SIB, 0),
        lambda: (score(SIB, 1), teacher(0)),
        lambda: (teacher(1), teacher(2)),
        lambda: teacher(3),
        lambda: teacher(4),
        all_teacher,
    ]
    per_step = -(-len(work) // CHUNKS)
    for i in range(CHUNKS + 1):
        if i < CHUNKS:
            g_y(i).wait_recv()
            g_z(i).start()

            @pl.when(fwd_y)
            def _():
                g_f(YB, i).start()

        if i >= 1:
            g_z(i - 1).wait_recv()

            @pl.when(jnp.logical_not(fwd_y))
            def _():
                g_f(ZB, i - 1).start()

        for f in work[i * per_step:(i + 1) * per_step]:
            f()
        if i == half - 1:
            score(YB, 0)
        if i == half:
            score(ZB, 0)
        if i == half + 1:
            for a in range(half):
                g_f(YB, a).wait_recv()
            score(FB, 0)
        if i == CHUNKS - 1:
            score(YB, 1)
    score(ZB, 1)
    for a in range(half, CHUNKS):
        g_f(YB, a).wait_recv()
    score(FB, 1)
    for i in range(CHUNKS):
        g_y(i).wait_send()
        g_sib(i).wait_send()
        g_z(i).wait_send()
        g_f(YB, i).wait_send()

    top = jnp.max(stat[0:8, :], axis=0, keepdims=True)

    def one(t, carry):
        z, d = carry
        r = pl.ds(pl.multiple_of((t % per) * strip, strip), strip)
        x = st[t // per, r, :] - top
        e = jnp.exp(x)
        st[t // per, r, :] = e
        return z + fold(e, jnp.sum), d + fold(tg[t // per, r, :] * x, jnp.sum)

    zero = jnp.zeros((8, rows), F32)
    zs, cross = lax.fori_loop(0, 5 * per, one, (zero, zero))
    zs = jnp.sum(zs, axis=0, keepdims=True)
    cross = jnp.sum(cross, axis=0, keepdims=True)
    zt = jnp.sum(stat[16:24, :], axis=0, keepdims=True)
    dt = jnp.sum(stat[24:32, :], axis=0, keepdims=True)
    loss[...] = (dt - cross) / zt - jnp.log(zt) + jnp.log(zs)
    ks, kt = scale / zs, scale / zt

    def make_grads(b, j):
        def one(t, _):
            r = pl.ds(pl.multiple_of(j * size + t * 64, 64), 64)
            h, l = split(st[b, r, :] * ks - tg[b, r, :] * kt)
            gh[b, r, :] = h
            gl[b, r, :] = l
            return 0
        lax.fori_loop(0, size // 64, one, 0)

    def weigh(b, j):
        make_grads(b, j)
        out = pg.at[group(j)] if b == OWN else win.at[b, group(j)]

        def one(t, _):
            c = pl.ds(pl.multiple_of(t * 256, 256), 256)
            out[:, c] = dot3(gh[b, group(j), :], gl[b, group(j), :], qh[:, c], ql[:, c], 1, 0)
            return 0
        lax.fori_loop(0, width // 256, one, 0)

    def add(dst, src, start, count):
        def one(t, _):
            r = pl.ds(pl.multiple_of(start + t * 16, 16), 16)
            dst[r, :] = dst[r, :] + src[r, :]
            return 0
        lax.fori_loop(0, count // 16, one, 0)

    for j in range(2):
        mine = range(j * half, (j + 1) * half)
        weigh(FB, j)
        for i in mine:
            t_f(i).start()
        weigh(ZB, j)

        @pl.when(z_gets)
        def _():
            for i in mine:
                t_f(i).wait_recv()
            add(win.at[ZB], rec.at[FB], j * size, size)

        for i in mine:
            t_z(i).start()
    for j in range(2):
        mine = range(j * half, (j + 1) * half)
        weigh(YB, j)

        @pl.when(jnp.logical_not(z_gets))
        def _():
            for i in mine:
                t_f(i).wait_recv()
            add(win.at[YB], rec.at[FB], j * size, size)

    def query_part(b, m):
        def one(t, _):
            c = pl.ds(pl.multiple_of(t * 256, 256), 256)
            x = dot3(gh[b, :, group(m)], gl[b, :, group(m)], wh[b, :, c], wl[b, :, c], 0, 0)
            if b == SIB:
                qg[group(m), c] = x
            else:
                qg[group(m), c] = qg[group(m), c] + x
            return 0
        lax.fori_loop(0, width // 256, one, 0)

    def sibling_out():
        for j in range(2):
            weigh(SIB, j)
            for i in range(j * half, (j + 1) * half):
                t_sib(i).start()

    def own_out():
        for j in range(2):
            weigh(OWN, j)

    def sibling_in():
        for i in range(CHUNKS):
            t_sib(i).wait_recv()
        add(pg, rec.at[SIB], 0, rows)

    work = [sibling_out, own_out] + [
        functools.partial(query_part, b, m) for b in range(5) for m in range(2)
    ]
    work.insert(4, sibling_in)
    per_step = -(-len(work) // CHUNKS)
    for i in range(CHUNKS + 1):
        if i < CHUNKS:
            t_z(i).wait_recv()
            add(win.at[YB], rec.at[ZB], i * step, step)
            t_y(i).start()
        for f in work[i * per_step:(i + 1) * per_step]:
            f()
        if i >= 1:
            t_y(i - 1).wait_recv()
            add(pg, rec.at[YB], (i - 1) * step, step)
    for i in range(CHUNKS):
        t_sib(i).wait_send()
        t_f(i).wait_send()
        t_z(i).wait_send()
        t_y(i).wait_send()


def body(n, queries, passages, pattern, teacher):
    rows, width = queries.shape
    vmem = pl.BlockSpec(memory_space=pltpu.VMEM)
    loss, query_grad, passage_grad = pl.pallas_call(
        functools.partial(kernel, n),
        out_shape=(
            jax.ShapeDtypeStruct((1, rows), F32),
            jax.ShapeDtypeStruct((rows, width), F32),
            jax.ShapeDtypeStruct((rows, width), F32),
        ),
        in_specs=[pl.BlockSpec(memory_space=pltpu.SMEM), vmem, vmem, vmem],
        out_specs=(vmem, vmem, vmem),
        scratch_shapes=[
            pltpu.VMEM((4, rows, width), F32),
            pltpu.VMEM((5, rows, width), BF16),
            pltpu.VMEM((5, rows, width), BF16),
            pltpu.VMEM((rows, width), BF16),
            pltpu.VMEM((rows, width), BF16),
            pltpu.VMEM((5, rows, rows), F32),
            pltpu.VMEM((5, rows, rows), F32),
            pltpu.VMEM((5, rows, rows), BF16),
            pltpu.VMEM((5, rows, rows), BF16),
            pltpu.VMEM((4, rows, width), F32),
            pltpu.VMEM((32, rows), F32),
            pltpu.SMEM((20,), jnp.int32),
            pltpu.SMEM((20,), F32),
            pltpu.SemaphoreType.DMA((4, CHUNKS)),
            pltpu.SemaphoreType.DMA((4, CHUNKS)),
            pltpu.SemaphoreType.DMA((4, CHUNKS)),
            pltpu.SemaphoreType.DMA((4, CHUNKS)),
        ],
        compiler_params=pltpu.CompilerParams(
            collective_id=0, has_side_effects=True, vmem_limit_bytes=60 * 2**20
        ),
    )(pattern, queries, passages, teacher)
    return loss.reshape(rows), query_grad, passage_grad


def solution(mesh):
    placed = (
        P(("grp", "blk"), None),
        P(("grp", "blk"), None),
        P(("grp", "blk"), None),
        P(("grp", "blk"), None, None, None),
    )
    return jax.shard_map(
        functools.partial(body, mesh.shape["blk"]),
        mesh=mesh,
        in_specs=placed,
        out_specs=(P(("grp", "blk")), P(("grp", "blk"), None), P(("grp", "blk"), None)),
        check_vma=False,
    )
```

```python
import functools
import math

import jax
import jax.numpy as jnp
from jax import lax
from jax.experimental import pallas as pl
from jax.experimental.pallas import tpu as pltpu
from jax.sharding import PartitionSpec as P

CHUNKS = 8
BANDS = 2
DEAD = -1e30
SIB, YB, ZB, FB, OWN = range(5)
F32 = jnp.float32
BF16 = jnp.bfloat16
MESH = pl.DeviceIdType.MESH


def split(x):
    hi = x.astype(BF16)
    return hi, (x - hi.astype(F32)).astype(BF16)


def dot(a, b, ca, cb):
    return lax.dot_general(a, b, (((ca,), (cb,)), ((), ())), preferred_element_type=F32)


def dot3(ah, al, bh, bl, ca, cb):
    return dot(ah, bh, ca, cb) + (dot(al, bh, ca, cb) + dot(ah, bl, ca, cb))


def fold(x, op):
    rows, cols = x.shape
    return op(x.reshape(rows // 8, 8, cols), axis=0)


def kernel(
    n, pat, qin, pin, tin, loss, qout, pout,
    q, p, teach, qg, pg,
    win, wh, wl, qh, ql, st, tg, gh, gl, rec, stat, kk, cap,
    s1, r1, s2, r2, ins, outs,
):
    rows, width = q.shape
    groups, slots, size, _ = teach.shape
    scale = 2.0 / math.sqrt(width)
    part = lax.axis_index("grp")
    me = lax.axis_index("blk")
    chip, core = me // 2, me % 2
    odd = chip % 2
    to = 1 - 2 * odd
    wrap = lambda i: lax.rem(i + n, n)
    sib = me + 1 - 2 * core
    ypart = me + 2 * to
    znext = wrap(me + 4 * to)
    zprev = wrap(me - 4 * to)
    owners = [sib, ypart, wrap(me - 2 * to), wrap(me + 2 * core - 1), me]
    fwd_y = core == odd
    z_gets = core != odd

    for i, (a, b) in enumerate(((pin, p), (qin, q), (tin, teach))):
        pltpu.make_async_copy(a, b, ins.at[i]).start()

    barrier = pltpu.get_barrier_semaphore()
    for d in (sib, ypart, znext, zprev):
        pl.semaphore_signal(barrier, inc=1, device_id=(part, d), device_id_type=MESH)
    pl.semaphore_wait(barrier, 4)

    def copy(src, dst, ss, rs, kind, i, dev):
        return pltpu.make_async_remote_copy(
            src_ref=src, dst_ref=dst, send_sem=ss.at[kind, i], recv_sem=rs.at[kind, i],
            device_id=(part, dev), device_id_type=MESH,
        )

    step = rows // CHUNKS
    quarter = CHUNKS // BANDS
    piece = lambda i: pl.ds(i * step, step)
    group = lambda j: pl.ds(j * size, size)
    band = rows // BANDS
    rows_of = lambda t: pl.ds(t * band, band)
    loaded = lambda i, a, b: pltpu.make_async_copy(a, b, ins.at[i]).wait()

    g_sib = lambda i: copy(pin.at[piece(i)], win.at[SIB, piece(i)], s1, r1, SIB, i, sib)
    g_y = lambda i: copy(pin.at[piece(i)], win.at[YB, piece(i)], s1, r1, YB, i, ypart)
    g_z = lambda i: copy(win.at[YB, piece(i)], win.at[ZB, piece(i)], s1, r1, ZB, i, znext)
    g_f = lambda b, i: copy(win.at[b, piece(i)], win.at[FB, piece(i)], s1, r1, FB, i, sib)
    t_sib = lambda i: copy(win.at[SIB, piece(i)], rec.at[SIB, piece(i)], s2, r2, SIB, i, sib)
    t_y = lambda i: copy(win.at[YB, piece(i)], rec.at[YB, piece(i)], s2, r2, YB, i, ypart)
    t_z = lambda i: copy(win.at[ZB, piece(i)], rec.at[ZB, piece(i)], s2, r2, ZB, i, zprev)
    t_f = lambda i: copy(win.at[FB, piece(i)], rec.at[FB, piece(i)], s2, r2, FB, i, sib)

    for i in range(CHUNKS):
        g_y(i).start()
    for i in range(CHUNKS):
        g_sib(i).start()

    for b in range(5):
        for j in range(2):
            wanted = owners[b] * 2 + j
            for g in range(groups):
                slot, live = jnp.int32(0), jnp.int32(0)
                for k in range(slots):
                    hit = (pat[g, k] == wanted).astype(jnp.int32)
                    slot = jnp.maximum(slot, hit * k)
                    live = jnp.maximum(live, hit)
                kk[(g * 5 + b) * 2 + j] = slot
                alive = live.astype(F32)
                cap[(g * 5 + b) * 2 + j] = 3e38 * alive + DEAD * (1.0 - alive)

    stat[...] = jnp.full(stat.shape, DEAD, F32)

    def split_rows(src, hi, lo, count, strip=32):
        def one(t, _):
            r = pl.ds(pl.multiple_of(t * strip, strip), strip)
            h, l = split(src[r, :])
            hi[r, :] = h
            lo[r, :] = l
            return 0
        lax.fori_loop(0, count // strip, one, 0)

    def score(b, t):
        j = t * band // size
        src = p.at[rows_of(t)] if b == OWN else win.at[b, rows_of(t)]
        split_rows(src, wh.at[b, rows_of(t)], wl.at[b, rows_of(t)], band)
        for g in range(groups):
            cols = pl.ds(g * size, size)
            s = dot3(wh[b, rows_of(t), :], wl[b, rows_of(t), :], qh[group(g), :], ql[group(g), :], 1, 1)
            s = jnp.minimum(s * scale, cap[(g * 5 + b) * 2 + j])
            st[b, rows_of(t), cols] = s
            stat[0:8, cols] = jnp.maximum(stat[0:8, cols], fold(s, jnp.max))

    def teacher(b, g):
        def one(j, _):
            at = (g * 5 + b) * 2 + j
            x = teach[g, kk[at]].astype(F32).T
            x = jnp.minimum(x, cap[at])
            r = pl.ds(pl.multiple_of(j * size, size), size)
            c = pl.ds(g * size, size)
            tg[b, r, c] = x
            stat[8:16, c] = jnp.maximum(stat[8:16, c], fold(x, jnp.max))
            return 0
        lax.fori_loop(0, 2, one, 0)

    strip = 64
    per = rows // strip

    def teacher_sums(b):
        top = jnp.max(stat[8:16, :], axis=0, keepdims=True)

        def one(t, carry):
            z, d = carry
            r = pl.ds(pl.multiple_of(t * strip, strip), strip)
            x = tg[b, r, :] - top
            e = jnp.exp(x)
            tg[b, r, :] = e
            return z + fold(e, jnp.sum), d + fold(e * x, jnp.sum)
        zero = jnp.zeros((8, rows), F32)
        z, d = lax.fori_loop(0, per, one, (zero, zero))
        if b:
            z, d = stat[16:24, :] + z, stat[24:32, :] + d
        stat[16:24, :] = z
        stat[24:32, :] = d

    def first():
        loaded(0, pin, p)
        loaded(1, qin, q)
        split_rows(q, qh, ql, rows)

    def sibling():
        for i in range(CHUNKS):
            g_sib(i).wait_recv()
        score(SIB, 0)

    work = [first] + [functools.partial(score, OWN, t) for t in range(BANDS)]
    work += [sibling] + [functools.partial(score, SIB, t) for t in range(1, BANDS)]
    work += [lambda: loaded(2, tin, teach)]
    work += [functools.partial(teacher, b, g) for b in range(5) for g in range(groups)]
    work += [functools.partial(teacher_sums, b) for b in range(5)]
    total = len(work)

    def forwarded(t):
        for a in range(t * quarter, (t + 1) * quarter):
            g_f(YB, a).wait_recv()
        score(FB, t)

    for i in range(CHUNKS + 1):
        if i < CHUNKS:
            g_y(i).wait_recv()
            g_z(i).start()

            @pl.when(fwd_y)
            def _():
                g_f(YB, i).start()

        if i >= 1:
            g_z(i - 1).wait_recv()

            @pl.when(jnp.logical_not(fwd_y))
            def _():
                g_f(ZB, i - 1).start()

        for f in work[min(i, CHUNKS - 1) * total // (CHUNKS - 1):min(i + 1, CHUNKS - 1) * total // (CHUNKS - 1)]:
            f()
        t, phase = divmod(i + 1, quarter)
        if phase == 0 and i < CHUNKS:
            score(YB, t - 1)
        if phase == 1 and t:
            score(ZB, t - 1)
        if phase == 2 and t:
            forwarded(t - 1)
    forwarded(BANDS - 1)
    for i in range(CHUNKS):
        g_y(i).wait_send()
        g_sib(i).wait_send()
        g_z(i).wait_send()
        g_f(YB, i).wait_send()

    top = jnp.max(stat[0:8, :], axis=0, keepdims=True)

    def one(t, carry):
        z, d = carry
        r = pl.ds(pl.multiple_of((t % per) * strip, strip), strip)
        x = st[t // per, r, :] - top
        e = jnp.exp(x)
        st[t // per, r, :] = e
        return z + fold(e, jnp.sum), d + fold(tg[t // per, r, :] * x, jnp.sum)

    zero = jnp.zeros((8, rows), F32)
    zs, cross = lax.fori_loop(0, 5 * per, one, (zero, zero))
    zs = jnp.sum(zs, axis=0, keepdims=True)
    cross = jnp.sum(cross, axis=0, keepdims=True)
    zt = jnp.sum(stat[16:24, :], axis=0, keepdims=True)
    dt = jnp.sum(stat[24:32, :], axis=0, keepdims=True)
    loss[...] = (dt - cross) / zt - jnp.log(zt) + jnp.log(zs)
    ks, kt = scale / zs, scale / zt

    def weigh(b, start, count):
        def grads(t, _):
            r = pl.ds(pl.multiple_of(start + t * 64, 64), 64)
            h, l = split(st[b, r, :] * ks - tg[b, r, :] * kt)
            gh[b, r, :] = h
            gl[b, r, :] = l
            return 0
        lax.fori_loop(0, count // 64, grads, 0)
        at = pl.ds(start, count)
        out = pg.at[at] if b == OWN else win.at[b, at]

        def one(t, _):
            c = pl.ds(pl.multiple_of(t * 256, 256), 256)
            out[:, c] = dot3(gh[b, at, :], gl[b, at, :], qh[:, c], ql[:, c], 1, 0)
            return 0
        lax.fori_loop(0, width // 256, one, 0)

    def add(dst, src, start, count):
        def one(t, _):
            r = pl.ds(pl.multiple_of(start + t * 16, 16), 16)
            dst[r, :] = dst[r, :] + src[r, :]
            return 0
        lax.fori_loop(0, count // 16, one, 0)

    for t in range(BANDS):
        mine = range(t * quarter, (t + 1) * quarter)
        weigh(FB, t * band, band)
        for i in mine:
            t_f(i).start()
        weigh(ZB, t * band, band)

        @pl.when(z_gets)
        def _():
            for i in mine:
                t_f(i).wait_recv()
            add(win.at[ZB], rec.at[FB], t * band, band)

        for i in mine:
            t_z(i).start()
        weigh(YB, t * band, band)

    @pl.when(jnp.logical_not(z_gets))
    def _():
        for i in range(CHUNKS):
            t_f(i).wait_recv()
        add(win.at[YB], rec.at[FB], 0, rows)

    def query_part(b, m, side):
        def one(t, _):
            c = pl.ds(pl.multiple_of(t * 256, 256), 256)
            x = dot3(gh[b, :, group(m)], gl[b, :, group(m)], wh[b, :, c], wl[b, :, c], 0, 0)
            if b == SIB:
                qg[group(m), c] = x
            else:
                qg[group(m), c] = qg[group(m), c] + x
            return 0
        tiles = width // 512
        lax.fori_loop(side * tiles, (side + 1) * tiles, one, 0)

    def sibling_out(j):
        weigh(SIB, j * size, size)
        for i in range(j * CHUNKS // 2, (j + 1) * CHUNKS // 2):
            t_sib(i).start()

    def sibling_in():
        for i in range(CHUNKS):
            t_sib(i).wait_recv()
        add(pg, rec.at[SIB], 0, rows)

    stored = lambda i: pltpu.make_async_copy(pg.at[piece(i)], pout.at[piece(i)], outs.at[i])
    query_stored = pltpu.make_async_copy(qg, qout, outs.at[CHUNKS])

    work = [functools.partial(sibling_out, j) for j in range(2)]
    work += [functools.partial(weigh, OWN, j * size, size) for j in range(2)]
    work += [sibling_in] + [
        functools.partial(query_part, b, m, side)
        for b in range(5) for m in range(groups) for side in range(2)
    ]
    work += [query_stored.start]
    total = len(work)
    lag = 2
    for i in range(CHUNKS + lag):
        if i < CHUNKS:
            t_z(i).wait_recv()
            add(win.at[YB], rec.at[ZB], i * step, step)
            t_y(i).start()
        if i < CHUNKS - 1:
            for f in work[i * total // (CHUNKS - 1):(i + 1) * total // (CHUNKS - 1)]:
                f()
        if i >= lag:
            t_y(i - lag).wait_recv()
            add(pg, rec.at[YB], (i - lag) * step, step)
            stored(i - lag).start()
    query_stored.wait()
    for i in range(CHUNKS):
        stored(i).wait()
    for i in range(CHUNKS):
        t_sib(i).wait_send()
        t_f(i).wait_send()
        t_z(i).wait_send()
        t_y(i).wait_send()


def body(n, queries, passages, pattern, teacher):
    rows, width = queries.shape
    vmem = pl.BlockSpec(memory_space=pltpu.VMEM)
    hbm = pl.BlockSpec(memory_space=pl.ANY)
    loss, query_grad, passage_grad = pl.pallas_call(
        functools.partial(kernel, n),
        out_shape=(
            jax.ShapeDtypeStruct((1, rows), F32),
            jax.ShapeDtypeStruct((rows, width), F32),
            jax.ShapeDtypeStruct((rows, width), F32),
        ),
        in_specs=[pl.BlockSpec(memory_space=pltpu.SMEM), hbm, hbm, hbm],
        out_specs=(vmem, hbm, hbm),
        scratch_shapes=[
            pltpu.VMEM((rows, width), F32),
            pltpu.VMEM((rows, width), F32),
            pltpu.VMEM(teacher.shape, BF16),
            pltpu.VMEM((rows, width), F32),
            pltpu.VMEM((rows, width), F32),
            pltpu.VMEM((4, rows, width), F32),
            pltpu.VMEM((5, rows, width), BF16),
            pltpu.VMEM((5, rows, width), BF16),
            pltpu.VMEM((rows, width), BF16),
            pltpu.VMEM((rows, width), BF16),
            pltpu.VMEM((5, rows, rows), F32),
            pltpu.VMEM((5, rows, rows), F32),
            pltpu.VMEM((5, rows, rows), BF16),
            pltpu.VMEM((5, rows, rows), BF16),
            pltpu.VMEM((4, rows, width), F32),
            pltpu.VMEM((32, rows), F32),
            pltpu.SMEM((20,), jnp.int32),
            pltpu.SMEM((20,), F32),
            pltpu.SemaphoreType.DMA((4, CHUNKS)),
            pltpu.SemaphoreType.DMA((4, CHUNKS)),
            pltpu.SemaphoreType.DMA((4, CHUNKS)),
            pltpu.SemaphoreType.DMA((4, CHUNKS)),
            pltpu.SemaphoreType.DMA((3,)),
            pltpu.SemaphoreType.DMA((CHUNKS + 1,)),
        ],
        compiler_params=pltpu.CompilerParams(
            collective_id=0, has_side_effects=True, vmem_limit_bytes=60 * 2**20
        ),
    )(pattern, queries, passages, teacher)
    return loss.reshape(rows), query_grad, passage_grad


def solution(mesh):
    placed = (
        P(("grp", "blk"), None),
        P(("grp", "blk"), None),
        P(("grp", "blk"), None),
        P(("grp", "blk"), None, None, None),
    )
    return jax.shard_map(
        functools.partial(body, mesh.shape["blk"]),
        mesh=mesh,
        in_specs=placed,
        out_specs=(P(("grp", "blk")), P(("grp", "blk"), None), P(("grp", "blk"), None)),
        check_vma=False,
    )
```
